512 devices in a mesh: row: 16 (over x_hi, y, core), col: 32 (over z, x_lo).
Axes of the slice: x: 4 (x_hi: 2, x_lo: 2; x = x_hi * 2 + x_lo), y: 4, z: 16, core: 2. Of those that a mesh axis runs over, the one named last changes fastest.
Arguments:
- coefficients: bfloat16 [32, 1048576], P(None, ('row', 'col')), may hold values from -6 to 6
- factors: bfloat16 [4, 16384, 128, 64], P(None, ('row', 'col')), may hold values from -0.5 to 0.5
- pattern: int32 [4, 16384], P(None, ('row', 'col')), may hold values from 0 to 31, as said below
- octree_order: int32 [16384], P(('row', 'col')), may hold values from 0 to 31, as said below
- panels: bfloat16 [32, 1048576], P(None, ('row', 'col')), may hold values from -6 to 6
- near_blocks: bfloat16 [16384, 6, 64, 64], P(('row', 'col')), may hold values from -0.3125 to 0.3125
- neighbors: int32 [16384, 6], P(('row', 'col')), may hold values from 0 to 16383, as said below
Outputs:
- far_field: bfloat16 [32, 1048576], P(None, ('row', 'col'))
- near_field: bfloat16 [32, 1048576], P(None, ('row', 'col'))
The draws below stay inside these ranges and needn't reach their ends.
Inputs may be any that keep to these rules, and one draw needn't show every extreme that they name: `pattern`: for every level, the entries of one device's 32 boxes are a permutation of 0 .. 31. `octree_order`: the entries of one device's 32 boxes are a permutation of 0 .. 31. `neighbors`: every entry lies within 32 of its own panel number g; entry 0 is g itself; entry 1 is g + 32 or g - 32, limited to 0 .. 16383.
All inputs are finite; a program needn't handle non-finite values.
Results may differ from the reference program's by a relative error of at most 0.0064.
Values may be sent and summed in bfloat16 or wider, within the bound.
No kernel may reach another device: no remote copies, remote signals or barrier semaphores. Data moves between devices by JAX's collectives and lax.ppermute only.
A program may use at most 64 MiB of HBM per device.

```python
import jax
import jax.numpy as jnp
from jax import lax

BOX_DEV = 32
R = 64
K = 32
P_SIZE = 64
NEAR = 6
LEVELS = 4
NB = 16384
N_ROW = 16
N_COL = 32


def block_permutations(key, count):
    keys = jax.random.split(key, count * (NB // BOX_DEV))
    perms = jax.vmap(lambda item: jax.random.permutation(item, BOX_DEV))(keys)
    return perms.astype(jnp.int32).reshape(count, NB)


def draw_pattern(key, part):
    key = jax.random.fold_in(key, 11)
    return block_permutations(key, LEVELS)


def draw_octree_order(key, part):
    key = jax.random.fold_in(key, 23)
    return block_permutations(key, 1).reshape(NB)


def draw_neighbors(key, part):
    key = jax.random.fold_in(key, 37)
    first_key, second_key = jax.random.split(key)
    own = jnp.arange(NB).astype(jnp.int32)[:, None]
    offsets = jax.random.randint(first_key, (NB, NEAR - 2), -BOX_DEV, BOX_DEV + 1).astype(jnp.int32)
    signs = jax.random.randint(second_key, (NB, 1), 0, 2).astype(jnp.int32) * 2 - 1
    joined = jnp.concatenate([own, own + signs * BOX_DEV, own + offsets], axis=1)
    return jnp.clip(joined, 0, NB - 1).astype(jnp.int32)


def levels(stream_key, extent, shards, low, largest):
    gain = 1.0
    for dim, blocks in shards:
        steps = jax.random.uniform(jax.random.fold_in(jax.random.fold_in(stream_key, 6), dim), (blocks,), jnp.float32, low / len(shards), largest / len(shards))
        gain = gain * jnp.repeat(jnp.exp(steps), extent[dim] // blocks).reshape((-1,) + (1,) * (len(extent) - 1 - dim))
    return gain


def centred(rng, extent, spread, bound, cuts=(), held_as=jnp.bfloat16):
    factor_of = levels(rng, extent, cuts, -0.22, 0.18) if cuts else 1.0
    drawn = jax.random.normal(rng, extent, jnp.float32) * spread * factor_of
    return jnp.minimum(jnp.maximum(drawn, -bound), bound).astype(held_as)


def setup_inputs(seed: int = 0) -> dict:
    streams_of = jax.random.split(jax.random.key(seed), 8)
    coefficients = centred(streams_of[0], (K, NB * R), 1.0, 6.0, ((1, 512),))
    factors = centred(streams_of[1], (LEVELS, NB, 2 * R, R), (2 * R) ** -0.5, 0.5, ((1, 512),))
    pattern = draw_pattern(jax.random.fold_in(streams_of[7], 71), 0)
    octree_order = draw_octree_order(jax.random.fold_in(streams_of[7], 71), 0)
    panels = centred(streams_of[4], (K, NB * P_SIZE), 1.0, 6.0, ((1, 512),))
    near_blocks = centred(streams_of[5], (NB, NEAR, P_SIZE, P_SIZE), (NEAR * P_SIZE) ** -0.5, 0.3125, ((0, 512),))
    neighbors = draw_neighbors(jax.random.fold_in(streams_of[7], 71), 0)
    return {"coefficients": coefficients, "factors": factors, "pattern": pattern, "octree_order": octree_order, "panels": panels, "near_blocks": near_blocks, "neighbors": neighbors}


def reference(coefficients, factors, pattern, octree_order, panels, near_blocks, neighbors):
    groups = N_ROW * N_COL
    blocks = coefficients.reshape(K, N_ROW, N_COL, BOX_DEV, R)
    layout = pattern.reshape(LEVELS, N_ROW, N_COL, BOX_DEV)
    matrices = factors.reshape(LEVELS, N_ROW, N_COL, BOX_DEV, 2 * R, R)
    for level in range(LEVELS):
        if level % 2 == 0:
            shift_bit = N_COL.bit_length() - 2 - level // 2
            other = jnp.arange(N_COL).astype(jnp.int32) ^ (1 << shift_bit)
            partner = blocks[:, :, other]
        else:
            shift_bit = N_ROW.bit_length() - 2 - level // 2
            other = jnp.arange(N_ROW).astype(jnp.int32) ^ (1 << shift_bit)
            partner = blocks[:, other]
        index = jnp.broadcast_to(layout[level][None, :, :, :, None], (K, N_ROW, N_COL, BOX_DEV, R))
        chosen = jnp.take_along_axis(partner, index, axis=3)
        stacked = jnp.concatenate([blocks, chosen], axis=4).astype(jnp.float32)
        blocks = jnp.einsum("krcbi,rcbio->krcbo", stacked, matrices[level].astype(jnp.float32)).astype(jnp.bfloat16)
    order = jnp.broadcast_to(octree_order.reshape(N_ROW, N_COL, BOX_DEV)[None, :, :, :, None], (K, N_ROW, N_COL, BOX_DEV, R))
    far_field = jnp.take_along_axis(blocks, order, axis=3).reshape(K, NB * R)
    boxes = panels.reshape(K, NB, P_SIZE)

    def one_group(pieces):
        index, local_blocks = pieces
        taken = boxes[:, index, :].astype(jnp.float32)
        return jnp.einsum("kbnp,bnpq->kbq", taken, local_blocks.astype(jnp.float32))

    summed = lax.map(one_group, (neighbors.reshape(groups, BOX_DEV, NEAR), near_blocks.reshape(groups, BOX_DEV, NEAR, P_SIZE, P_SIZE)))
    near_field = jnp.transpose(summed, (1, 0, 2, 3)).reshape(K, NB * P_SIZE).astype(jnp.bfloat16)
    return far_field, near_field
```

```python
import functools

import jax
import jax.numpy as jnp
from jax import lax
from jax.experimental import pallas as pl
from jax.experimental.pallas import tpu as pltpu
from jax.sharding import PartitionSpec as P

LANES = 128
NT = (((1,), (1,)), ((), ()))


def exchange(value, axis, mask):
    pairs = [(i, i ^ mask) for i in range(lax.axis_size(axis))]
    return lax.ppermute(value, axis, pairs)


def tile_of(ref, box):
    start = pl.multiple_of((box >> 1) * LANES, LANES)
    return ref[:, pl.ds(start, LANES)]


def placed(tile, box, upper):
    half = box & 1
    shift = (1 - half if upper else half) * (LANES // 2)
    return pltpu.roll(tile, shift, 1)


def level_body(level, ordered, pattern, order, own, partner, matrices, out):
    rows = own.shape[0]
    boxes = matrices.shape[0]
    low = lax.broadcasted_iota(jnp.int32, (rows, LANES), 1) < LANES // 2
    for pair in range(boxes // 2):
        sides = []
        weights = []
        for g in (2 * pair, 2 * pair + 1):
            box = order[g] if ordered else g
            if ordered:
                mine = placed(tile_of(own, box), box, False)
            else:
                mine = own[:, pair * LANES : (pair + 1) * LANES]
                if g & 1:
                    mine = pltpu.roll(mine, LANES // 2, 1)
            q = pattern[level, box]
            theirs = placed(tile_of(partner, q), q, True)
            sides.append(jnp.where(low, mine, theirs))
            weights.append(matrices[box])
        product = lax.dot_general(
            jnp.concatenate(sides, axis=0),
            jnp.concatenate(weights, axis=0),
            NT,
            preferred_element_type=jnp.float32,
        )
        joined = jnp.where(low, product[:rows], product[rows:])
        out[:, pair * LANES : (pair + 1) * LANES] = joined.astype(out.dtype)


def combine(level, ordered, pattern, order, own, partner, matrices):
    _, boxes, rank, depth = matrices.shape
    smem = pl.BlockSpec(memory_space=pltpu.SMEM)
    vmem = pl.BlockSpec(memory_space=pltpu.VMEM)
    return pl.pallas_call(
        functools.partial(level_body, level, ordered),
        grid=(1,),
        out_shape=jax.ShapeDtypeStruct(own.shape, own.dtype),
        in_specs=[
            smem,
            smem,
            vmem,
            vmem,
            pl.BlockSpec((None, boxes, rank, depth), lambda i: (level, 0, 0, 0)),
        ],
        out_specs=vmem,
        cost_estimate=pl.CostEstimate(
            flops=2 * own.size * depth, bytes_accessed=1 << 20, transcendentals=0
        ),
        name=f"level{level}",
    )(pattern, order, own, partner, matrices)


def near_body(first, neighbors, before, own, after, matrices, out, held):
    rows = own.shape[0]
    boxes, near, width, _ = matrices.shape
    tiles = own.shape[1] // LANES
    for part, source in enumerate((before, own, after)):
        for t in range(tiles):
            tile = source[:, t * LANES : (t + 1) * LANES]
            held[0, part * tiles + t] = tile
            held[1, part * tiles + t] = pltpu.roll(tile, LANES // 2, 1)
    low = lax.broadcasted_iota(jnp.int32, (rows, LANES), 1) < LANES // 2
    base = first[0]
    for pair in range(boxes // 2):
        sums = []
        for g in (2 * pair, 2 * pair + 1):
            sides = []
            for n in range(0, near, 2):
                a = neighbors[n, g] - base
                b = neighbors[n + 1, g] - base
                lower = held[a & 1, a >> 1]
                upper = held[1 - (b & 1), b >> 1]
                sides.append(jnp.where(low, lower, upper))
            sums.append(
                jnp.dot(
                    jnp.concatenate(sides, axis=1),
                    matrices[g].reshape(near * width, width),
                    preferred_element_type=jnp.float32,
                )
            )
        joined = jnp.concatenate(sums, axis=1).astype(out.dtype)
        out[:, pair * LANES : (pair + 1) * LANES] = joined


def near_sums(first, neighbors, before, own, after, matrices):
    smem = pl.BlockSpec(memory_space=pltpu.SMEM)
    vmem = pl.BlockSpec(memory_space=pltpu.VMEM)
    rows, columns = own.shape
    return pl.pallas_call(
        near_body,
        out_shape=jax.ShapeDtypeStruct(own.shape, own.dtype),
        in_specs=[smem, smem, vmem, vmem, vmem, vmem],
        out_specs=vmem,
        scratch_shapes=[pltpu.VMEM((2, 3 * columns // LANES, rows, LANES), own.dtype)],
        cost_estimate=pl.CostEstimate(
            flops=2 * own.size * 384, bytes_accessed=4 << 20, transcendentals=0
        ),
        name="near",
    )(first, neighbors, before, own, after, matrices)


def per_device(coefficients, factors, pattern, octree_order, panels, near_blocks, neighbors):
    boxes = pattern.shape[1]
    col_bits = lax.axis_size("col").bit_length() - 1
    row_bits = lax.axis_size("row").bit_length() - 1
    matrices = jnp.swapaxes(factors, 2, 3)
    blocks = coefficients
    levels = factors.shape[0]
    for level in range(levels):
        if level % 2 == 0:
            partner = exchange(blocks, "col", 1 << (col_bits - 1 - level // 2))
        else:
            partner = exchange(blocks, "row", 1 << (row_bits - 1 - level // 2))
        blocks = combine(
            level, level == levels - 1, pattern, octree_order, blocks, partner, matrices
        )
    both = ("row", "col")
    count = lax.axis_size(both)
    up = [(i, i + 1) for i in range(count - 1)]
    down = [(j, i) for i, j in up]
    before = lax.ppermute(panels, both, up)
    after = lax.ppermute(panels, both, down)
    first = (lax.axis_index(both) * boxes - boxes).astype(jnp.int32).reshape(1)
    near_field = near_sums(
        first, jnp.swapaxes(neighbors, 0, 1), before, panels, after, near_blocks
    )
    return (blocks, near_field)


def solution(mesh):
    in_specs = (
        P(None, ("row", "col")),
        P(None, ("row", "col"), None, None),
        P(None, ("row", "col")),
        P(("row", "col")),
        P(None, ("row", "col")),
        P(("row", "col"), None, None, None),
        P(("row", "col"), None),
    )
    out_specs = (P(None, ("row", "col")), P(None, ("row", "col")))
    return jax.shard_map(
        per_device, mesh=mesh, in_specs=in_specs, out_specs=out_specs, check_vma=False
    )
```

```python
import functools

import jax
import jax.numpy as jnp
from jax import lax
from jax.experimental import pallas as pl
from jax.experimental.pallas import tpu as pltpu
from jax.sharding import PartitionSpec as P

LANES = 128
MIB = 1 << 20
NT = (((1,), (1,)), ((), ()))


def exchange(value, axis, mask):
    pairs = [(i, i ^ mask) for i in range(lax.axis_size(axis))]
    return lax.ppermute(value, axis, pairs)


def tile_of(ref, box):
    start = pl.multiple_of((box >> 1) * LANES, LANES)
    return ref[:, pl.ds(start, LANES)]


def placed(tile, box, upper):
    half = box & 1
    shift = (1 - half if upper else half) * (LANES // 2)
    return pltpu.roll(tile, shift, 1)


def level_body(level, ordered, pattern, order, own, partner, matrices, out):
    rows = own.shape[0]
    boxes = matrices.shape[0]
    low = lax.broadcasted_iota(jnp.int32, (rows, LANES), 1) < LANES // 2
    for pair in range(boxes // 2):
        sides = []
        weights = []
        for g in (2 * pair, 2 * pair + 1):
            box = order[g] if ordered else g
            if ordered:
                mine = placed(tile_of(own, box), box, False)
            else:
                mine = own[:, pair * LANES : (pair + 1) * LANES]
                if g & 1:
                    mine = pltpu.roll(mine, LANES // 2, 1)
            q = pattern[level, box]
            theirs = placed(tile_of(partner, q), q, True)
            sides.append(jnp.where(low, mine, theirs))
            weights.append(matrices[box])
        product = lax.dot_general(
            jnp.concatenate(sides, axis=0),
            jnp.concatenate(weights, axis=0),
            NT,
            preferred_element_type=jnp.float32,
        )
        joined = jnp.where(low, product[:rows], product[rows:])
        out[:, pair * LANES : (pair + 1) * LANES] = joined.astype(out.dtype)


def combine(level, ordered, pattern, order, own, partner, matrices):
    _, boxes, rank, depth = matrices.shape
    smem = pl.BlockSpec(memory_space=pltpu.SMEM)
    vmem = pl.BlockSpec(memory_space=pltpu.VMEM)
    return pl.pallas_call(
        functools.partial(level_body, level, ordered),
        grid=(1,),
        out_shape=jax.ShapeDtypeStruct(own.shape, own.dtype),
        in_specs=[
            smem,
            smem,
            vmem,
            vmem,
            pl.BlockSpec((None, boxes, rank, depth), lambda i: (level, 0, 0, 0)),
        ],
        out_specs=vmem,
        cost_estimate=pl.CostEstimate(
            flops=2 * own.size * depth, bytes_accessed=1 << 20, transcendentals=0
        ),
        compiler_params=pltpu.CompilerParams(vmem_limit_bytes=4 * MIB),
        name=f"level{level}",
    )(pattern, order, own, partner, matrices)


def stage_body(*refs):
    count = (len(refs) - 1) // 2
    sources, targets, sems = refs[:count], refs[count : 2 * count], refs[-1]
    copies = [
        pltpu.make_async_copy(source, target, sems.at[i])
        for i, (source, target) in enumerate(zip(sources, targets))
    ]
    for copy in copies:
        copy.start()
    for copy in copies:
        copy.wait()


def staged(*arrays):
    hbm = pl.BlockSpec(memory_space=pltpu.HBM)
    vmem = pl.BlockSpec(memory_space=pltpu.VMEM)
    size = sum(a.size * a.dtype.itemsize for a in arrays)
    return pl.pallas_call(
        stage_body,
        out_shape=[jax.ShapeDtypeStruct(a.shape, a.dtype) for a in arrays],
        in_specs=[hbm] * len(arrays),
        out_specs=[vmem] * len(arrays),
        scratch_shapes=[pltpu.SemaphoreType.DMA((len(arrays),))],
        cost_estimate=pl.CostEstimate(flops=0, bytes_accessed=2 * size, transcendentals=0),
        compiler_params=pltpu.CompilerParams(vmem_limit_bytes=8 * MIB),
        name="stage",
    )(*(pltpu.with_memory_space_constraint(a, pltpu.HBM) for a in arrays))


def near_body(first, neighbors, before, own, after, matrices, out, held):
    rows = own.shape[0]
    boxes, near, width, _ = matrices.shape
    tiles = own.shape[1] // LANES
    for part, source in enumerate((before, own, after)):
        for t in range(tiles):
            tile = source[:, t * LANES : (t + 1) * LANES]
            held[0, part * tiles + t] = tile
            held[1, part * tiles + t] = pltpu.roll(tile, LANES // 2, 1)
    low = lax.broadcasted_iota(jnp.int32, (rows, LANES), 1) < LANES // 2
    base = first[0]
    for pair in range(boxes // 2):
        sums = []
        for g in (2 * pair, 2 * pair + 1):
            sides = []
            for n in range(0, near, 2):
                a = neighbors[n, g] - base
                b = neighbors[n + 1, g] - base
                lower = held[a & 1, a >> 1]
                upper = held[1 - (b & 1), b >> 1]
                sides.append(jnp.where(low, lower, upper))
            sums.append(
                jnp.dot(
                    jnp.concatenate(sides, axis=1),
                    matrices[g].reshape(near * width, width),
                    preferred_element_type=jnp.float32,
                )
            )
        joined = jnp.concatenate(sums, axis=1).astype(out.dtype)
        out[:, pair * LANES : (pair + 1) * LANES] = joined


def near_sums(first, neighbors, before, own, after, matrices):
    smem = pl.BlockSpec(memory_space=pltpu.SMEM)
    vmem = pl.BlockSpec(memory_space=pltpu.VMEM)
    rows, columns = own.shape
    return pl.pallas_call(
        near_body,
        out_shape=jax.ShapeDtypeStruct(own.shape, own.dtype),
        in_specs=[smem, smem, vmem, vmem, vmem, vmem],
        out_specs=vmem,
        scratch_shapes=[pltpu.VMEM((2, 3 * columns // LANES, rows, LANES), own.dtype)],
        cost_estimate=pl.CostEstimate(
            flops=2 * own.size * 384, bytes_accessed=4 << 20, transcendentals=0
        ),
        compiler_params=pltpu.CompilerParams(vmem_limit_bytes=8 * MIB),
        name="near",
    )(first, neighbors, before, own, after, matrices)


def per_device(coefficients, factors, pattern, octree_order, panels, near_blocks, neighbors):
    boxes = pattern.shape[1]
    col_bits = lax.axis_size("col").bit_length() - 1
    row_bits = lax.axis_size("row").bit_length() - 1
    both = ("row", "col")
    count = lax.axis_size(both)
    up = [(i, i + 1) for i in range(count - 1)]
    down = [(j, i) for i, j in up]
    partner = exchange(coefficients, "col", 1 << (col_bits - 1))
    before = lax.ppermute(panels, both, up)
    after = lax.ppermute(panels, both, down)
    matrices = jnp.swapaxes(factors, 2, 3)
    blocks, matrices, pattern, octree_order = staged(
        coefficients, matrices, pattern, octree_order
    )
    levels = factors.shape[0]
    for level in range(levels):
        if level == 0:
            pass
        elif level % 2 == 0:
            partner = exchange(blocks, "col", 1 << (col_bits - 1 - level // 2))
        else:
            partner = exchange(blocks, "row", 1 << (row_bits - 1 - level // 2))
        blocks = combine(
            level, level == levels - 1, pattern, octree_order, blocks, partner, matrices
        )
    first = (lax.axis_index(both) * boxes - boxes).astype(jnp.int32).reshape(1)
    near_field = near_sums(
        first, jnp.swapaxes(neighbors, 0, 1), before, panels, after, near_blocks
    )
    return (blocks, near_field)


def solution(mesh):
    in_specs = (
        P(None, ("row", "col")),
        P(None, ("row", "col"), None, None),
        P(None, ("row", "col")),
        P(("row", "col")),
        P(None, ("row", "col")),
        P(("row", "col"), None, None, None),
        P(("row", "col"), None),
    )
    out_specs = (P(None, ("row", "col")), P(None, ("row", "col")))
    return jax.shard_map(
        per_device, mesh=mesh, in_specs=in_specs, out_specs=out_specs, check_vma=False
    )
```

```python
import functools

import jax
import jax.numpy as jnp
from jax import lax
from jax.experimental import pallas as pl
from jax.experimental.pallas import tpu as pltpu
from jax.sharding import PartitionSpec as P

LANES = 128
MIB = 1 << 20
NT = (((1,), (1,)), ((), ()))


def exchange(value, axis, mask):
    pairs = [(i, i ^ mask) for i in range(lax.axis_size(axis))]
    return lax.ppermute(value, axis, pairs)


def tile_of(ref, box):
    start = pl.multiple_of((box >> 1) * LANES, LANES)
    return ref[:, pl.ds(start, LANES)]


def placed(tile, box, upper):
    half = box & 1
    shift = (1 - half if upper else half) * (LANES // 2)
    return pltpu.roll(tile, shift, 1)


def level_body(level, ordered, pattern, order, own, partner, matrices, out):
    rows = own.shape[0]
    boxes = matrices.shape[1]
    low = lax.broadcasted_iota(jnp.int32, (rows, LANES), 1) < LANES // 2
    for pair in range(boxes // 2):
        sides = []
        weights = []
        for g in (2 * pair, 2 * pair + 1):
            box = order[g] if ordered else g
            if ordered:
                mine = placed(tile_of(own, box), box, False)
            else:
                mine = own[:, pair * LANES : (pair + 1) * LANES]
                if g & 1:
                    mine = pltpu.roll(mine, LANES // 2, 1)
            q = pattern[level, box]
            theirs = placed(tile_of(partner, q), q, True)
            sides.append(jnp.where(low, mine, theirs))
            weights.append(matrices[level, box])
        product = lax.dot_general(
            jnp.concatenate(sides, axis=0),
            jnp.concatenate(weights, axis=0),
            NT,
            preferred_element_type=jnp.float32,
        )
        joined = jnp.where(low, product[:rows], product[rows:])
        out[:, pair * LANES : (pair + 1) * LANES] = joined.astype(out.dtype)


def combine(level, ordered, pattern, order, own, partner, matrices):
    depth = matrices.shape[3]
    smem = pl.BlockSpec(memory_space=pltpu.SMEM)
    vmem = pl.BlockSpec(memory_space=pltpu.VMEM)
    return pl.pallas_call(
        functools.partial(level_body, level, ordered),
        out_shape=jax.ShapeDtypeStruct(own.shape, own.dtype),
        in_specs=[smem, smem, vmem, vmem, vmem],
        out_specs=vmem,
        cost_estimate=pl.CostEstimate(
            flops=2 * own.size * depth, bytes_accessed=1 << 20, transcendentals=0
        ),
        compiler_params=pltpu.CompilerParams(vmem_limit_bytes=4 * MIB),
        name=f"level{level}",
    )(pattern, order, own, partner, matrices)


def stage_body(*refs):
    count = (len(refs) - 1) // 2
    sources, targets, sems = refs[:count], refs[count : 2 * count], refs[-1]
    copies = [
        pltpu.make_async_copy(source, target, sems.at[i])
        for i, (source, target) in enumerate(zip(sources, targets))
    ]
    for copy in copies:
        copy.start()
    for copy in copies:
        copy.wait()


def staged(indices, arrays):
    hbm = pl.BlockSpec(memory_space=pltpu.HBM)
    smem = pl.BlockSpec(memory_space=pltpu.SMEM)
    vmem = pl.BlockSpec(memory_space=pltpu.VMEM)
    size = sum(a.size * a.dtype.itemsize for a in arrays)
    total = len(indices) + len(arrays)
    return pl.pallas_call(
        stage_body,
        out_shape=[pltpu.SMEM(a.shape, a.dtype) for a in indices]
        + [jax.ShapeDtypeStruct(a.shape, a.dtype) for a in arrays],
        in_specs=[hbm] * total,
        out_specs=[smem] * len(indices) + [vmem] * len(arrays),
        scratch_shapes=[pltpu.SemaphoreType.DMA((total,))],
        cost_estimate=pl.CostEstimate(flops=0, bytes_accessed=2 * size, transcendentals=0),
        compiler_params=pltpu.CompilerParams(vmem_limit_bytes=8 * MIB),
        name="stage",
    )(*(pltpu.with_memory_space_constraint(a, pltpu.HBM) for a in (*indices, *arrays)))


def near_body(place, neighbors, paired, own, inside, across, matrices, out, held):
    rows = own.shape[0]
    boxes, near, width, _ = matrices.shape
    tiles = own.shape[1] // LANES
    bits = boxes.bit_length() - 1
    from_across = place[2] != 0
    for part, source in enumerate((paired, own, inside)):
        for t in range(tiles):
            tile = source[:, t * LANES : (t + 1) * LANES]
            if part == 2:
                tile = jnp.where(from_across, across[:, t * LANES : (t + 1) * LANES], tile)
            held[0, part * tiles + t] = tile
            held[1, part * tiles + t] = pltpu.roll(tile, LANES // 2, 1)
    low = lax.broadcasted_iota(jnp.int32, (rows, LANES), 1) < LANES // 2
    base, direction = place[0], place[1]

    def found(n, g):
        offset = neighbors[n, g] - base
        slot = 1 + (offset >> bits) * direction
        return slot * tiles + ((offset & (boxes - 1)) >> 1), offset & 1

    for pair in range(boxes // 2):
        sums = []
        for g in (2 * pair, 2 * pair + 1):
            sides = []
            for n in range(0, near, 2):
                a, a_half = found(n, g)
                b, b_half = found(n + 1, g)
                lower = held[a_half, a]
                upper = held[1 - b_half, b]
                sides.append(jnp.where(low, lower, upper))
            sums.append(
                jnp.dot(
                    jnp.concatenate(sides, axis=1),
                    matrices[g].reshape(near * width, width),
                    preferred_element_type=jnp.float32,
                )
            )
        joined = jnp.concatenate(sums, axis=1).astype(out.dtype)
        out[:, pair * LANES : (pair + 1) * LANES] = joined


def near_sums(place, neighbors, paired, own, inside, across, matrices):
    smem = pl.BlockSpec(memory_space=pltpu.SMEM)
    vmem = pl.BlockSpec(memory_space=pltpu.VMEM)
    rows, columns = own.shape
    return pl.pallas_call(
        near_body,
        out_shape=jax.ShapeDtypeStruct(own.shape, own.dtype),
        in_specs=[smem, smem, vmem, vmem, vmem, vmem, vmem],
        out_specs=vmem,
        scratch_shapes=[pltpu.VMEM((2, 3 * columns // LANES, rows, LANES), own.dtype)],
        cost_estimate=pl.CostEstimate(
            flops=2 * own.size * 384, bytes_accessed=4 << 20, transcendentals=0
        ),
        compiler_params=pltpu.CompilerParams(vmem_limit_bytes=8 * MIB),
        name="near",
    )(place, neighbors, paired, own, inside, across, matrices)


def per_device(coefficients, factors, pattern, octree_order, panels, near_blocks, neighbors):
    boxes = pattern.shape[1]
    columns = lax.axis_size("col")
    col_bits = columns.bit_length() - 1
    row_bits = lax.axis_size("row").bit_length() - 1
    both = ("row", "col")
    count = lax.axis_size(both)
    tie = lax.optimization_barrier
    me = lax.axis_index(both).astype(jnp.int32)

    def crosses(i):
        return (i + 1) % (columns // 2) == 0

    def swaps(kept):
        odd = [i for i in range(1, count - 1, 2) if kept(i)]
        return [(i, i + 1) for i in odd] + [(i + 1, i) for i in odd]

    partner = exchange(coefficients, "col", 1 << (col_bits - 1))
    paired = lax.ppermute(panels, both, [(i, i ^ 1) for i in range(count)])
    across = lax.ppermute(panels, both, swaps(crosses))
    half = columns // 2
    at_edge = jnp.where(me & 1 == 1, (me + 1) % half, me % half) == 0
    place = jnp.stack([me * boxes, 2 * (me & 1) - 1, at_edge.astype(jnp.int32)])
    pattern, octree_order, neighbors, place, blocks, matrices = staged(
        (pattern, octree_order, jnp.swapaxes(neighbors, 0, 1), place),
        (coefficients, jnp.swapaxes(factors, 2, 3)),
    )

    def level(index, blocks, partner, last=False):
        return combine(index, last, pattern, octree_order, blocks, partner, matrices)

    blocks = level(0, blocks, partner)
    partner = exchange(blocks, "row", 1 << (row_bits - 1))
    partner, paired, across = tie((partner, paired, across))
    blocks = level(1, blocks, partner)
    partner = exchange(blocks, "col", 1 << (col_bits - 2))
    blocks, panels, near_blocks = tie((blocks, panels, near_blocks))
    (near_blocks,) = staged((), (near_blocks,))
    partner, near_blocks = tie((partner, near_blocks))
    inside = lax.ppermute(panels, both, swaps(lambda i: not crosses(i)))
    near_field = near_sums(
        place,
        neighbors,
        paired,
        panels,
        inside,
        across,
        near_blocks,
    )
    blocks = level(2, blocks, partner)
    partner = exchange(blocks, "row", 1 << (row_bits - 2))
    blocks = level(3, blocks, partner, True)
    return (blocks, near_field)


def solution(mesh):
    in_specs = (
        P(None, ("row", "col")),
        P(None, ("row", "col"), None, None),
        P(None, ("row", "col")),
        P(("row", "col")),
        P(None, ("row", "col")),
        P(("row", "col"), None, None, None),
        P(("row", "col"), None),
    )
    out_specs = (P(None, ("row", "col")), P(None, ("row", "col")))
    return jax.shard_map(
        per_device, mesh=mesh, in_specs=in_specs, out_specs=out_specs, check_vma=False
    )
```

```python
import functools

import jax
import jax.numpy as jnp
from jax import lax
from jax.experimental import pallas as pl
from jax.experimental.pallas import tpu as pltpu
from jax.sharding import PartitionSpec as P

LANES = 128
MIB = 1 << 20
NT = (((1,), (1,)), ((), ()))


def exchange(value, axis, mask):
    pairs = [(i, i ^ mask) for i in range(lax.axis_size(axis))]
    return lax.ppermute(value, axis, pairs)


def tile_of(ref, box):
    start = pl.multiple_of((box >> 1) * LANES, LANES)
    return ref[:, pl.ds(start, LANES)]


def placed(tile, box, upper):
    half = box & 1
    shift = (1 - half if upper else half) * (LANES // 2)
    return pltpu.roll(tile, shift, 1)


def level_body(level, ordered, pattern, order, own, partner, matrices, out):
    rows = own.shape[0]
    boxes = matrices.shape[1]
    low = lax.broadcasted_iota(jnp.int32, (rows, LANES), 1) < LANES // 2
    for pair in range(boxes // 2):
        sides = []
        weights = []
        for g in (2 * pair, 2 * pair + 1):
            box = order[g] if ordered else g
            if ordered:
                mine = placed(tile_of(own, box), box, False)
            else:
                mine = own[:, pair * LANES : (pair + 1) * LANES]
                if g & 1:
                    mine = pltpu.roll(mine, LANES // 2, 1)
            q = pattern[level, box]
            theirs = placed(tile_of(partner, q), q, True)
            sides.append(jnp.where(low, mine, theirs))
            weights.append(matrices[level, box])
        product = lax.dot_general(
            jnp.concatenate(sides, axis=0),
            jnp.concatenate(weights, axis=0),
            NT,
            preferred_element_type=jnp.float32,
        )
        joined = jnp.where(low, product[:rows], product[rows:])
        out[:, pair * LANES : (pair + 1) * LANES] = joined.astype(out.dtype)


def combine(level, ordered, pattern, order, own, partner, matrices):
    depth = matrices.shape[3]
    smem = pl.BlockSpec(memory_space=pltpu.SMEM)
    vmem = pl.BlockSpec(memory_space=pltpu.VMEM)
    return pl.pallas_call(
        functools.partial(level_body, level, ordered),
        out_shape=jax.ShapeDtypeStruct(own.shape, own.dtype),
        in_specs=[smem, smem, vmem, vmem, vmem],
        out_specs=vmem,
        cost_estimate=pl.CostEstimate(
            flops=2 * own.size * depth, bytes_accessed=1 << 20, transcendentals=0
        ),
        compiler_params=pltpu.CompilerParams(vmem_limit_bytes=4 * MIB),
        name=f"level{level}",
    )(pattern, order, own, partner, matrices)


def stage_body(*refs):
    count = (len(refs) - 1) // 2
    sources, targets, sems = refs[:count], refs[count : 2 * count], refs[-1]
    copies = [
        pltpu.make_async_copy(source, target, sems.at[i])
        for i, (source, target) in enumerate(zip(sources, targets))
    ]
    for copy in copies:
        copy.start()
    for copy in copies:
        copy.wait()


def staged(indices, arrays):
    hbm = pl.BlockSpec(memory_space=pltpu.HBM)
    smem = pl.BlockSpec(memory_space=pltpu.SMEM)
    vmem = pl.BlockSpec(memory_space=pltpu.VMEM)
    size = sum(a.size * a.dtype.itemsize for a in arrays)
    total = len(indices) + len(arrays)
    return pl.pallas_call(
        stage_body,
        out_shape=[pltpu.SMEM(a.shape, a.dtype) for a in indices]
        + [jax.ShapeDtypeStruct(a.shape, a.dtype) for a in arrays],
        in_specs=[hbm] * total,
        out_specs=[smem] * len(indices) + [vmem] * len(arrays),
        scratch_shapes=[pltpu.SemaphoreType.DMA((total,))],
        cost_estimate=pl.CostEstimate(flops=0, bytes_accessed=2 * size, transcendentals=0),
        compiler_params=pltpu.CompilerParams(vmem_limit_bytes=8 * MIB),
        name="stage",
    )(*(pltpu.with_memory_space_constraint(a, pltpu.HBM) for a in (*indices, *arrays)))


def near_body(neighbors, paired, own, inside, across, matrices, out, held):
    rows = own.shape[0]
    boxes, near, width, _ = matrices.shape
    tiles = own.shape[1] // LANES
    bits = boxes.bit_length() - 1
    base = neighbors[0, 0]
    direction = 2 * ((base >> bits) & 1) - 1
    for part, source in enumerate((paired, own, inside)):
        for t in range(tiles):
            tile = source[:, t * LANES : (t + 1) * LANES]
            if part == 2:
                tile = tile + across[:, t * LANES : (t + 1) * LANES]
            held[0, part * tiles + t] = tile
            held[1, part * tiles + t] = pltpu.roll(tile, LANES // 2, 1)
    low = lax.broadcasted_iota(jnp.int32, (rows, LANES), 1) < LANES // 2
    def found(n, g):
        offset = neighbors[n, g] - base
        slot = 1 + (offset >> bits) * direction
        return slot * tiles + ((offset & (boxes - 1)) >> 1), offset & 1

    for pair in range(boxes // 2):
        sums = []
        for g in (2 * pair, 2 * pair + 1):
            sides = []
            for n in range(0, near, 2):
                a, a_half = found(n, g)
                b, b_half = found(n + 1, g)
                lower = held[a_half, a]
                upper = held[1 - b_half, b]
                sides.append(jnp.where(low, lower, upper))
            sums.append(
                jnp.dot(
                    jnp.concatenate(sides, axis=1),
                    matrices[g].reshape(near * width, width),
                    preferred_element_type=jnp.float32,
                )
            )
        joined = jnp.concatenate(sums, axis=1).astype(out.dtype)
        out[:, pair * LANES : (pair + 1) * LANES] = joined


def near_sums(neighbors, paired, own, inside, across, matrices):
    smem = pl.BlockSpec(memory_space=pltpu.SMEM)
    vmem = pl.BlockSpec(memory_space=pltpu.VMEM)
    rows, columns = own.shape
    return pl.pallas_call(
        near_body,
        out_shape=jax.ShapeDtypeStruct(own.shape, own.dtype),
        in_specs=[smem, vmem, vmem, vmem, vmem, vmem],
        out_specs=vmem,
        scratch_shapes=[pltpu.VMEM((2, 3 * columns // LANES, rows, LANES), own.dtype)],
        cost_estimate=pl.CostEstimate(
            flops=2 * own.size * 384, bytes_accessed=4 << 20, transcendentals=0
        ),
        compiler_params=pltpu.CompilerParams(vmem_limit_bytes=8 * MIB),
        name="near",
    )(neighbors, paired, own, inside, across, matrices)


def per_device(coefficients, factors, pattern, octree_order, panels, near_blocks, neighbors):
    boxes = pattern.shape[1]
    columns = lax.axis_size("col")
    col_bits = columns.bit_length() - 1
    row_bits = lax.axis_size("row").bit_length() - 1
    both = ("row", "col")
    count = lax.axis_size(both)
    tie = lax.optimization_barrier

    def crosses(i):
        return (i + 1) % (columns // 2) == 0

    def swaps(kept):
        odd = [i for i in range(1, count - 1, 2) if kept(i)]
        return [(i, i + 1) for i in odd] + [(i + 1, i) for i in odd]

    partner = exchange(coefficients, "col", 1 << (col_bits - 1))
    across = lax.ppermute(panels, both, swaps(crosses))
    pattern, octree_order, neighbors, blocks, matrices, near_blocks = staged(
        (pattern, octree_order, jnp.swapaxes(neighbors, 0, 1)),
        (coefficients, jnp.swapaxes(factors, 2, 3), near_blocks),
    )

    def level(index, blocks, partner, last=False):
        return combine(index, last, pattern, octree_order, blocks, partner, matrices)

    blocks = level(0, blocks, partner)
    partner = exchange(blocks, "row", 1 << (row_bits - 1))
    partner, across = tie((partner, across))
    blocks = level(1, blocks, partner)
    partner = exchange(blocks, "col", 1 << (col_bits - 2))
    blocks, panels = tie((blocks, panels))
    paired = lax.ppermute(panels, both, [(i, i ^ 1) for i in range(count)])
    inside = lax.ppermute(panels, both, swaps(lambda i: not crosses(i)))
    near_field = near_sums(
        neighbors,
        paired,
        panels,
        inside,
        across,
        near_blocks,
    )
    blocks = level(2, blocks, partner)
    partner = exchange(blocks, "row", 1 << (row_bits - 2))
    blocks = level(3, blocks, partner, True)
    return (blocks, near_field)


def solution(mesh):
    in_specs = (
        P(None, ("row", "col")),
        P(None, ("row", "col"), None, None),
        P(None, ("row", "col")),
        P(("row", "col")),
        P(None, ("row", "col")),
        P(("row", "col"), None, None, None),
        P(("row", "col"), None),
    )
    out_specs = (P(None, ("row", "col")), P(None, ("row", "col")))
    return jax.shard_map(
        per_device, mesh=mesh, in_specs=in_specs, out_specs=out_specs, check_vma=False
    )
```

```python
import functools

import jax
import jax.numpy as jnp
from jax import lax
from jax.experimental import pallas as pl
from jax.experimental.pallas import tpu as pltpu
from jax.sharding import PartitionSpec as P

LANES = 128
MIB = 1 << 20
NT = (((1,), (1,)), ((), ()))


def exchange(value, axis, mask):
    pairs = [(i, i ^ mask) for i in range(lax.axis_size(axis))]
    return lax.ppermute(value, axis, pairs)


def exchange_pairs(value, axis, mask):
    pairs = [[i, i ^ mask] for i in range(lax.axis_size(axis)) if not i & mask]
    return lax.all_gather(value, axis, axis_index_groups=pairs)


def tile_of(ref, box):
    start = pl.multiple_of((box >> 1) * LANES, LANES)
    return ref[:, pl.ds(start, LANES)]


def placed(tile, box, upper):
    half = box & 1
    shift = (1 - half if upper else half) * (LANES // 2)
    return pltpu.roll(tile, shift, 1)


def level_body(level, ordered, bit, pattern, order, neighbors, own, partner, matrices, out):
    if bit is not None:
        partner = partner.at[1 - ((neighbors[0, 0] >> bit) & 1)]
    rows = own.shape[0]
    boxes = matrices.shape[1]
    low = lax.broadcasted_iota(jnp.int32, (rows, LANES), 1) < LANES // 2
    for pair in range(boxes // 2):
        sides = []
        weights = []
        for g in (2 * pair, 2 * pair + 1):
            box = order[g] if ordered else g
            if ordered:
                mine = placed(tile_of(own, box), box, False)
            else:
                mine = own[:, pair * LANES : (pair + 1) * LANES]
                if g & 1:
                    mine = pltpu.roll(mine, LANES // 2, 1)
            q = pattern[level, box]
            theirs = placed(tile_of(partner, q), q, True)
            sides.append(jnp.where(low, mine, theirs))
            weights.append(matrices[level, box])
        product = lax.dot_general(
            jnp.concatenate(sides, axis=0),
            jnp.concatenate(weights, axis=0),
            NT,
            preferred_element_type=jnp.float32,
        )
        joined = jnp.where(low, product[:rows], product[rows:])
        out[:, pair * LANES : (pair + 1) * LANES] = joined.astype(out.dtype)


def combine(level, ordered, bit, pattern, order, neighbors, own, partner, matrices):
    depth = matrices.shape[3]
    smem = pl.BlockSpec(memory_space=pltpu.SMEM)
    vmem = pl.BlockSpec(memory_space=pltpu.VMEM)
    return pl.pallas_call(
        functools.partial(level_body, level, ordered, bit),
        out_shape=jax.ShapeDtypeStruct(own.shape, own.dtype),
        in_specs=[smem, smem, smem, vmem, vmem, vmem],
        out_specs=vmem,
        cost_estimate=pl.CostEstimate(
            flops=2 * own.size * depth, bytes_accessed=1 << 20, transcendentals=0
        ),
        compiler_params=pltpu.CompilerParams(vmem_limit_bytes=4 * MIB),
        name=f"level{level}",
    )(pattern, order, neighbors, own, partner, matrices)


def stage_body(*refs):
    count = (len(refs) - 1) // 2
    sources, targets, sems = refs[:count], refs[count : 2 * count], refs[-1]
    copies = [
        pltpu.make_async_copy(source, target, sems.at[i])
        for i, (source, target) in enumerate(zip(sources, targets))
    ]
    for copy in copies:
        copy.start()
    for copy in copies:
        copy.wait()


def staged(indices, arrays):
    hbm = pl.BlockSpec(memory_space=pltpu.HBM)
    smem = pl.BlockSpec(memory_space=pltpu.SMEM)
    vmem = pl.BlockSpec(memory_space=pltpu.VMEM)
    size = sum(a.size * a.dtype.itemsize for a in arrays)
    total = len(indices) + len(arrays)
    return pl.pallas_call(
        stage_body,
        out_shape=[pltpu.SMEM(a.shape, a.dtype) for a in indices]
        + [jax.ShapeDtypeStruct(a.shape, a.dtype) for a in arrays],
        in_specs=[hbm] * total,
        out_specs=[smem] * len(indices) + [vmem] * len(arrays),
        scratch_shapes=[pltpu.SemaphoreType.DMA((total,))],
        cost_estimate=pl.CostEstimate(flops=0, bytes_accessed=2 * size, transcendentals=0),
        compiler_params=pltpu.CompilerParams(vmem_limit_bytes=8 * MIB),
        name="stage",
    )(*(pltpu.with_memory_space_constraint(a, pltpu.HBM) for a in (*indices, *arrays)))


def near_body(neighbors, paired, own, inside, across, matrices, out, held):
    rows = own.shape[0]
    boxes, near, width, _ = matrices.shape
    tiles = own.shape[1] // LANES
    bits = boxes.bit_length() - 1
    base = neighbors[0, 0]
    direction = 2 * ((base >> bits) & 1) - 1
    for part, source in enumerate((paired, own, inside)):
        for t in range(tiles):
            tile = source[:, t * LANES : (t + 1) * LANES]
            if part == 2:
                tile = tile + across[:, t * LANES : (t + 1) * LANES]
            held[0, part * tiles + t] = tile
            held[1, part * tiles + t] = pltpu.roll(tile, LANES // 2, 1)
    low = lax.broadcasted_iota(jnp.int32, (rows, LANES), 1) < LANES // 2
    def found(n, g):
        offset = neighbors[n, g] - base
        slot = 1 + (offset >> bits) * direction
        return slot * tiles + ((offset & (boxes - 1)) >> 1), offset & 1

    for pair in range(boxes // 2):
        sums = []
        for g in (2 * pair, 2 * pair + 1):
            sides = []
            for n in range(0, near, 2):
                a, a_half = found(n, g)
                b, b_half = found(n + 1, g)
                lower = held[a_half, a]
                upper = held[1 - b_half, b]
                sides.append(jnp.where(low, lower, upper))
            sums.append(
                jnp.dot(
                    jnp.concatenate(sides, axis=1),
                    matrices[g].reshape(near * width, width),
                    preferred_element_type=jnp.float32,
                )
            )
        joined = jnp.concatenate(sums, axis=1).astype(out.dtype)
        out[:, pair * LANES : (pair + 1) * LANES] = joined


def last_body(level, bit, pattern, order, neighbors, own, gathered, matrices, *refs):
    paired, panels, inside, across, near_blocks, far_out, near_out, held = refs
    level_body(level, True, bit, pattern, order, neighbors, own, gathered, matrices, far_out)
    near_body(neighbors, paired, panels, inside, across, near_blocks, near_out, held)


def last_and_near(level, bit, indices, own, gathered, matrices, halos, near_blocks):
    smem = pl.BlockSpec(memory_space=pltpu.SMEM)
    vmem = pl.BlockSpec(memory_space=pltpu.VMEM)
    rows, columns = own.shape
    out = jax.ShapeDtypeStruct(own.shape, own.dtype)
    return pl.pallas_call(
        functools.partial(last_body, level, bit),
        out_shape=[out, out],
        in_specs=[smem] * 3 + [vmem] * 8,
        out_specs=[vmem, vmem],
        scratch_shapes=[pltpu.VMEM((2, 3 * columns // LANES, rows, LANES), own.dtype)],
        cost_estimate=pl.CostEstimate(
            flops=2 * own.size * 512, bytes_accessed=5 << 20, transcendentals=0
        ),
        compiler_params=pltpu.CompilerParams(vmem_limit_bytes=8 * MIB),
        name="last",
    )(*indices, own, gathered, matrices, *halos, near_blocks)


def per_device(coefficients, factors, pattern, octree_order, panels, near_blocks, neighbors):
    boxes = pattern.shape[1]
    columns = lax.axis_size("col")
    col_bits = columns.bit_length() - 1
    row_bits = lax.axis_size("row").bit_length() - 1
    both = ("row", "col")
    count = lax.axis_size(both)
    tie = lax.optimization_barrier

    def crosses(i):
        return (i + 1) % (columns // 2) == 0

    def swaps(kept):
        odd = [i for i in range(1, count - 1, 2) if kept(i)]
        return [(i, i + 1) for i in odd] + [(i + 1, i) for i in odd]

    partner = exchange(coefficients, "col", 1 << (col_bits - 1))
    across = lax.ppermute(panels, both, swaps(crosses))
    pattern, octree_order, neighbors, blocks, matrices, near_blocks = staged(
        (pattern, octree_order, jnp.swapaxes(neighbors, 0, 1)),
        (coefficients, jnp.swapaxes(factors, 2, 3), near_blocks),
    )

    def level(index, blocks, partner, last=False, bit=None):
        return combine(
            index, last, bit, pattern, octree_order, neighbors, blocks, partner, matrices
        )

    blocks = level(0, blocks, partner)
    gathered = exchange_pairs(blocks, "row", 1 << (row_bits - 1))
    gathered, across = tie((gathered, across))
    own_bit = boxes.bit_length() - 1 + col_bits
    blocks = level(1, blocks, gathered, bit=own_bit + row_bits - 1)
    partner = exchange(blocks, "col", 1 << (col_bits - 2))
    blocks, panels = tie((blocks, panels))
    paired = lax.ppermute(panels, both, [(i, i ^ 1) for i in range(count)])
    inside = lax.ppermute(panels, both, swaps(lambda i: not crosses(i)))
    blocks = level(2, blocks, partner)
    gathered = exchange_pairs(blocks, "row", 1 << (row_bits - 2))
    return last_and_near(
        3,
        own_bit + row_bits - 2,
        (pattern, octree_order, neighbors),
        blocks,
        gathered,
        matrices,
        (paired, panels, inside, across),
        near_blocks,
    )


def solution(mesh):
    in_specs = (
        P(None, ("row", "col")),
        P(None, ("row", "col"), None, None),
        P(None, ("row", "col")),
        P(("row", "col")),
        P(None, ("row", "col")),
        P(("row", "col"), None, None, None),
        P(("row", "col"), None),
    )
    out_specs = (P(None, ("row", "col")), P(None, ("row", "col")))
    return jax.shard_map(
        per_device, mesh=mesh, in_specs=in_specs, out_specs=out_specs, check_vma=False
    )
```

```python
import functools

import jax
import jax.numpy as jnp
from jax import lax
from jax.experimental import pallas as pl
from jax.experimental.pallas import tpu as pltpu
from jax.sharding import PartitionSpec as P

LANES = 128
MIB = 1 << 20
NT = (((1,), (1,)), ((), ()))


def exchange(value, axis, mask):
    pairs = [(i, i ^ mask) for i in range(lax.axis_size(axis))]
    return lax.ppermute(value, axis, pairs)


def exchange_pairs(value, axis, mask):
    pairs = [[i, i ^ mask] for i in range(lax.axis_size(axis)) if not i & mask]
    return lax.all_gather(value, axis, axis_index_groups=pairs)


def tile_of(ref, box):
    start = pl.multiple_of((box >> 1) * LANES, LANES)
    return ref[:, pl.ds(start, LANES)]


def placed(tile, box, upper):
    half = box & 1
    shift = (1 - half if upper else half) * (LANES // 2)
    return pltpu.roll(tile, shift, 1)


def level_body(level, ordered, bit, pattern, order, neighbors, own, partner, matrices, out):
    if bit is not None:
        partner = partner.at[1 - ((neighbors[0, 0] >> bit) & 1)]
    rows = own.shape[0]
    boxes = matrices.shape[1]
    low = lax.broadcasted_iota(jnp.int32, (rows, LANES), 1) < LANES // 2
    for pair in range(boxes // 2):
        sides = []
        weights = []
        for g in (2 * pair, 2 * pair + 1):
            box = order[g] if ordered else g
            if ordered:
                mine = placed(tile_of(own, box), box, False)
            else:
                mine = own[:, pair * LANES : (pair + 1) * LANES]
                if g & 1:
                    mine = pltpu.roll(mine, LANES // 2, 1)
            q = pattern[level, box]
            theirs = placed(tile_of(partner, q), q, True)
            sides.append(jnp.where(low, mine, theirs))
            weights.append(matrices[level, box])
        product = lax.dot_general(
            jnp.concatenate(sides, axis=0),
            jnp.concatenate(weights, axis=0),
            NT,
            preferred_element_type=jnp.float32,
        )
        joined = jnp.where(low, product[:rows], product[rows:])
        out[:, pair * LANES : (pair + 1) * LANES] = joined.astype(out.dtype)


def combine(level, ordered, bit, pattern, order, neighbors, own, partner, matrices):
    depth = matrices.shape[3]
    smem = pl.BlockSpec(memory_space=pltpu.SMEM)
    vmem = pl.BlockSpec(memory_space=pltpu.VMEM)
    return pl.pallas_call(
        functools.partial(level_body, level, ordered, bit),
        out_shape=jax.ShapeDtypeStruct(own.shape, own.dtype),
        in_specs=[smem, smem, smem, vmem, vmem, vmem],
        out_specs=vmem,
        cost_estimate=pl.CostEstimate(
            flops=2 * own.size * depth, bytes_accessed=1 << 20, transcendentals=0
        ),
        compiler_params=pltpu.CompilerParams(vmem_limit_bytes=4 * MIB),
        name=f"level{level}",
    )(pattern, order, neighbors, own, partner, matrices)


def stage_body(*refs):
    count = (len(refs) - 1) // 2
    sources, targets, sems = refs[:count], refs[count : 2 * count], refs[-1]
    copies = [
        pltpu.make_async_copy(source, target, sems.at[i])
        for i, (source, target) in enumerate(zip(sources, targets))
    ]
    for copy in copies:
        copy.start()
    for copy in copies:
        copy.wait()


def staged(indices, arrays):
    hbm = pl.BlockSpec(memory_space=pltpu.HBM)
    smem = pl.BlockSpec(memory_space=pltpu.SMEM)
    vmem = pl.BlockSpec(memory_space=pltpu.VMEM)
    size = sum(a.size * a.dtype.itemsize for a in arrays)
    total = len(indices) + len(arrays)
    return pl.pallas_call(
        stage_body,
        out_shape=[pltpu.SMEM(a.shape, a.dtype) for a in indices]
        + [jax.ShapeDtypeStruct(a.shape, a.dtype) for a in arrays],
        in_specs=[hbm] * total,
        out_specs=[smem] * len(indices) + [vmem] * len(arrays),
        scratch_shapes=[pltpu.SemaphoreType.DMA((total,))],
        cost_estimate=pl.CostEstimate(flops=0, bytes_accessed=2 * size, transcendentals=0),
        compiler_params=pltpu.CompilerParams(vmem_limit_bytes=8 * MIB),
        name="stage",
    )(*(pltpu.with_memory_space_constraint(a, pltpu.HBM) for a in (*indices, *arrays)))


def near_body(neighbors, paired, own, inside, wrapped, across, matrices, out, held):
    rows = own.shape[0]
    boxes, near, width, _ = matrices.shape
    tiles = own.shape[1] // LANES
    bits = boxes.bit_length() - 1
    base = neighbors[0, 0]
    direction = 2 * ((base >> bits) & 1) - 1
    for part, source in enumerate((paired, own, inside)):
        for t in range(tiles):
            tile = source[:, t * LANES : (t + 1) * LANES]
            if part == 2:
                tile = tile + wrapped[:, t * LANES : (t + 1) * LANES]
                tile = tile + across[:, t * LANES : (t + 1) * LANES]
            held[0, part * tiles + t] = tile
            held[1, part * tiles + t] = pltpu.roll(tile, LANES // 2, 1)
    low = lax.broadcasted_iota(jnp.int32, (rows, LANES), 1) < LANES // 2
    def found(n, g):
        offset = neighbors[n, g] - base
        slot = 1 + (offset >> bits) * direction
        return slot * tiles + ((offset & (boxes - 1)) >> 1), offset & 1

    for pair in range(boxes // 2):
        sums = []
        for g in (2 * pair, 2 * pair + 1):
            sides = []
            for n in range(0, near, 2):
                a, a_half = found(n, g)
                b, b_half = found(n + 1, g)
                lower = held[a_half, a]
                upper = held[1 - b_half, b]
                sides.append(jnp.where(low, lower, upper))
            sums.append(
                jnp.dot(
                    jnp.concatenate(sides, axis=1),
                    matrices[g].reshape(near * width, width),
                    preferred_element_type=jnp.float32,
                )
            )
        joined = jnp.concatenate(sums, axis=1).astype(out.dtype)
        out[:, pair * LANES : (pair + 1) * LANES] = joined


def last_body(level, bit, pattern, order, neighbors, own, gathered, matrices, *refs):
    paired, panels, inside, wrapped, across, near_blocks, far_out, near_out, held = refs
    level_body(level, True, bit, pattern, order, neighbors, own, gathered, matrices, far_out)
    near_body(
        neighbors, paired, panels, inside, wrapped, across, near_blocks, near_out, held
    )


def last_and_near(level, bit, indices, own, gathered, matrices, halos, near_blocks):
    smem = pl.BlockSpec(memory_space=pltpu.SMEM)
    vmem = pl.BlockSpec(memory_space=pltpu.VMEM)
    rows, columns = own.shape
    out = jax.ShapeDtypeStruct(own.shape, own.dtype)
    return pl.pallas_call(
        functools.partial(last_body, level, bit),
        out_shape=[out, out],
        in_specs=[smem] * 3 + [vmem] * 9,
        out_specs=[vmem, vmem],
        scratch_shapes=[pltpu.VMEM((2, 3 * columns // LANES, rows, LANES), own.dtype)],
        cost_estimate=pl.CostEstimate(
            flops=2 * own.size * 512, bytes_accessed=5 << 20, transcendentals=0
        ),
        compiler_params=pltpu.CompilerParams(vmem_limit_bytes=8 * MIB),
        name="last",
    )(*indices, own, gathered, matrices, *halos, near_blocks)


def per_device(coefficients, factors, pattern, octree_order, panels, near_blocks, neighbors):
    boxes = pattern.shape[1]
    columns = lax.axis_size("col")
    col_bits = columns.bit_length() - 1
    row_bits = lax.axis_size("row").bit_length() - 1
    both = ("row", "col")
    count = lax.axis_size(both)
    tie = lax.optimization_barrier

    def crosses(i):
        return (i + 1) % (columns // 2) == 0

    def wraps(i):
        return (i + 1) % (2 * columns) == columns

    def swaps(kept):
        odd = [i for i in range(1, count - 1, 2) if kept(i)]
        return [(i, i + 1) for i in odd] + [(i + 1, i) for i in odd]

    partner = exchange(coefficients, "col", 1 << (col_bits - 1))
    wrapped = lax.ppermute(panels, both, swaps(wraps))
    pattern, octree_order, neighbors, blocks, matrices, near_blocks = staged(
        (pattern, octree_order, jnp.swapaxes(neighbors, 0, 1)),
        (coefficients, jnp.swapaxes(factors, 2, 3), near_blocks),
    )

    def level(index, blocks, partner, last=False, bit=None):
        return combine(
            index, last, bit, pattern, octree_order, neighbors, blocks, partner, matrices
        )

    blocks = level(0, blocks, partner)
    gathered = exchange_pairs(blocks, "row", 1 << (row_bits - 1))
    gathered, wrapped = tie((gathered, wrapped))
    own_bit = boxes.bit_length() - 1 + col_bits
    blocks = level(1, blocks, gathered, bit=own_bit + row_bits - 1)
    partner = exchange(blocks, "col", 1 << (col_bits - 2))
    blocks, panels = tie((blocks, panels))
    paired = lax.ppermute(panels, both, [(i, i ^ 1) for i in range(count)])
    inside = lax.ppermute(panels, both, swaps(lambda i: not crosses(i)))
    across = lax.ppermute(panels, both, swaps(lambda i: crosses(i) and not wraps(i)))
    blocks = level(2, blocks, partner)
    gathered = exchange_pairs(blocks, "row", 1 << (row_bits - 2))
    return last_and_near(
        3,
        own_bit + row_bits - 2,
        (pattern, octree_order, neighbors),
        blocks,
        gathered,
        matrices,
        (paired, panels, inside, wrapped, across),
        near_blocks,
    )


def solution(mesh):
    in_specs = (
        P(None, ("row", "col")),
        P(None, ("row", "col"), None, None),
        P(None, ("row", "col")),
        P(("row", "col")),
        P(None, ("row", "col")),
        P(("row", "col"), None, None, None),
        P(("row", "col"), None),
    )
    out_specs = (P(None, ("row", "col")), P(None, ("row", "col")))
    return jax.shard_map(
        per_device, mesh=mesh, in_specs=in_specs, out_specs=out_specs, check_vma=False
    )
```

```python
import functools

import jax
import jax.numpy as jnp
from jax import lax
from jax.experimental import pallas as pl
from jax.experimental.pallas import tpu as pltpu
from jax.sharding import PartitionSpec as P

LANES = 128
MIB = 1 << 20
NT = (((1,), (1,)), ((), ()))


def exchange(value, axis, mask):
    pairs = [(i, i ^ mask) for i in range(lax.axis_size(axis))]
    return lax.ppermute(value, axis, pairs)


def exchange_pairs(value, axis, mask):
    pairs = [[i, i ^ mask] for i in range(lax.axis_size(axis)) if not i & mask]
    return lax.all_gather(value, axis, axis_index_groups=pairs)


def tile_of(ref, box):
    start = pl.multiple_of((box >> 1) * LANES, LANES)
    return ref[:, pl.ds(start, LANES)]


def placed(tile, box, upper):
    half = box & 1
    shift = (1 - half if upper else half) * (LANES // 2)
    return pltpu.roll(tile, shift, 1)


def level_body(level, ordered, bit, pattern, order, neighbors, own, partner, matrices, out):
    if bit is not None:
        partner = partner.at[1 - ((neighbors[0, 0] >> bit) & 1)]
    rows = own.shape[0]
    boxes = matrices.shape[1]
    low = lax.broadcasted_iota(jnp.int32, (rows, LANES), 1) < LANES // 2
    for pair in range(boxes // 2):
        sides = []
        weights = []
        for g in (2 * pair, 2 * pair + 1):
            box = order[g] if ordered else g
            if ordered:
                mine = placed(tile_of(own, box), box, False)
            else:
                mine = own[:, pair * LANES : (pair + 1) * LANES]
                if g & 1:
                    mine = pltpu.roll(mine, LANES // 2, 1)
            q = pattern[level, box]
            theirs = placed(tile_of(partner, q), q, True)
            sides.append(jnp.where(low, mine, theirs))
            weights.append(matrices[level, box])
        product = lax.dot_general(
            jnp.concatenate(sides, axis=0),
            jnp.concatenate(weights, axis=0),
            NT,
            preferred_element_type=jnp.float32,
        )
        joined = jnp.where(low, product[:rows], product[rows:])
        out[:, pair * LANES : (pair + 1) * LANES] = joined.astype(out.dtype)


def combine(level, ordered, bit, pattern, order, neighbors, own, partner, matrices):
    depth = matrices.shape[3]
    smem = pl.BlockSpec(memory_space=pltpu.SMEM)
    vmem = pl.BlockSpec(memory_space=pltpu.VMEM)
    return pl.pallas_call(
        functools.partial(level_body, level, ordered, bit),
        out_shape=jax.ShapeDtypeStruct(own.shape, own.dtype),
        in_specs=[smem, smem, smem, vmem, vmem, vmem],
        out_specs=vmem,
        cost_estimate=pl.CostEstimate(
            flops=2 * own.size * depth, bytes_accessed=1 << 20, transcendentals=0
        ),
        compiler_params=pltpu.CompilerParams(vmem_limit_bytes=4 * MIB),
        name=f"level{level}",
    )(pattern, order, neighbors, own, partner, matrices)


def stage_body(*refs):
    count = (len(refs) - 1) // 2
    sources, targets, sems = refs[:count], refs[count : 2 * count], refs[-1]
    copies = [
        pltpu.make_async_copy(source, target, sems.at[i])
        for i, (source, target) in enumerate(zip(sources, targets))
    ]
    for copy in copies:
        copy.start()
    for copy in copies:
        copy.wait()


def staged(indices, arrays):
    hbm = pl.BlockSpec(memory_space=pltpu.HBM)
    smem = pl.BlockSpec(memory_space=pltpu.SMEM)
    vmem = pl.BlockSpec(memory_space=pltpu.VMEM)
    size = sum(a.size * a.dtype.itemsize for a in arrays)
    total = len(indices) + len(arrays)
    return pl.pallas_call(
        stage_body,
        out_shape=[pltpu.SMEM(a.shape, a.dtype) for a in indices]
        + [jax.ShapeDtypeStruct(a.shape, a.dtype) for a in arrays],
        in_specs=[hbm] * total,
        out_specs=[smem] * len(indices) + [vmem] * len(arrays),
        scratch_shapes=[pltpu.SemaphoreType.DMA((total,))],
        cost_estimate=pl.CostEstimate(flops=0, bytes_accessed=2 * size, transcendentals=0),
        compiler_params=pltpu.CompilerParams(vmem_limit_bytes=8 * MIB),
        name="stage",
    )(*(pltpu.with_memory_space_constraint(a, pltpu.HBM) for a in (*indices, *arrays)))


def near_body(neighbors, early, paired, own, inside, wrapped, across, matrices, out, held):
    rows = own.shape[0]
    boxes, near, width, _ = matrices.shape
    tiles = own.shape[1] // LANES
    bits = boxes.bit_length() - 1
    base = neighbors[0, 0]
    direction = 2 * ((base >> bits) & 1) - 1
    for part, source in enumerate((paired, own, inside)):
        for t in range(tiles):
            tile = source[:, t * LANES : (t + 1) * LANES]
            if part == 0:
                tile = tile + early[:, t * LANES : (t + 1) * LANES]
            if part == 2:
                tile = tile + wrapped[:, t * LANES : (t + 1) * LANES]
                tile = tile + across[:, t * LANES : (t + 1) * LANES]
            held[0, part * tiles + t] = tile
            held[1, part * tiles + t] = pltpu.roll(tile, LANES // 2, 1)
    low = lax.broadcasted_iota(jnp.int32, (rows, LANES), 1) < LANES // 2
    def found(n, g):
        offset = neighbors[n, g] - base
        slot = 1 + (offset >> bits) * direction
        return slot * tiles + ((offset & (boxes - 1)) >> 1), offset & 1

    for pair in range(boxes // 2):
        sums = []
        for g in (2 * pair, 2 * pair + 1):
            sides = []
            for n in range(0, near, 2):
                a, a_half = found(n, g)
                b, b_half = found(n + 1, g)
                lower = held[a_half, a]
                upper = held[1 - b_half, b]
                sides.append(jnp.where(low, lower, upper))
            sums.append(
                jnp.dot(
                    jnp.concatenate(sides, axis=1),
                    matrices[g].reshape(near * width, width),
                    preferred_element_type=jnp.float32,
                )
            )
        joined = jnp.concatenate(sums, axis=1).astype(out.dtype)
        out[:, pair * LANES : (pair + 1) * LANES] = joined


def last_body(level, bit, pattern, order, neighbors, own, gathered, matrices, *refs):
    early, paired, panels, inside, wrapped, across, near_blocks, far_out, near_out, held = refs
    level_body(level, True, bit, pattern, order, neighbors, own, gathered, matrices, far_out)
    near_body(
        neighbors, early, paired, panels, inside, wrapped, across, near_blocks, near_out, held
    )


def last_and_near(level, bit, indices, own, gathered, matrices, halos, near_blocks):
    smem = pl.BlockSpec(memory_space=pltpu.SMEM)
    vmem = pl.BlockSpec(memory_space=pltpu.VMEM)
    rows, columns = own.shape
    out = jax.ShapeDtypeStruct(own.shape, own.dtype)
    return pl.pallas_call(
        functools.partial(last_body, level, bit),
        out_shape=[out, out],
        in_specs=[smem] * 3 + [vmem] * 10,
        out_specs=[vmem, vmem],
        scratch_shapes=[pltpu.VMEM((2, 3 * columns // LANES, rows, LANES), own.dtype)],
        cost_estimate=pl.CostEstimate(
            flops=2 * own.size * 512, bytes_accessed=5 << 20, transcendentals=0
        ),
        compiler_params=pltpu.CompilerParams(vmem_limit_bytes=8 * MIB),
        name="last",
    )(*indices, own, gathered, matrices, *halos, near_blocks)


def per_device(coefficients, factors, pattern, octree_order, panels, near_blocks, neighbors):
    boxes = pattern.shape[1]
    columns = lax.axis_size("col")
    col_bits = columns.bit_length() - 1
    row_bits = lax.axis_size("row").bit_length() - 1
    both = ("row", "col")
    count = lax.axis_size(both)
    tie = lax.optimization_barrier

    def crosses(i):
        return (i + 1) % (columns // 2) == 0

    def wraps(i):
        return (i + 1) % (2 * columns) == columns

    def swaps(kept):
        odd = [i for i in range(1, count - 1, 2) if kept(i)]
        return [(i, i + 1) for i in odd] + [(i + 1, i) for i in odd]

    partner = exchange(coefficients, "col", 1 << (col_bits - 1))
    wrapped = lax.ppermute(panels, both, swaps(wraps))

    def waits(i):
        return i % columns >= columns // 2 or i % columns // 2 in (1, 4, 6)

    early = lax.ppermute(panels, both, [(i, i ^ 1) for i in range(count) if waits(i)])
    pattern, octree_order, neighbors, blocks, matrices, near_blocks = staged(
        (pattern, octree_order, jnp.swapaxes(neighbors, 0, 1)),
        (coefficients, jnp.swapaxes(factors, 2, 3), near_blocks),
    )

    def level(index, blocks, partner, last=False, bit=None):
        return combine(
            index, last, bit, pattern, octree_order, neighbors, blocks, partner, matrices
        )

    blocks = level(0, blocks, partner)
    gathered = exchange_pairs(blocks, "row", 1 << (row_bits - 1))
    gathered, wrapped, early = tie((gathered, wrapped, early))
    own_bit = boxes.bit_length() - 1 + col_bits
    blocks = level(1, blocks, gathered, bit=own_bit + row_bits - 1)
    partner = exchange(blocks, "col", 1 << (col_bits - 2))
    blocks, panels = tie((blocks, panels))
    paired = lax.ppermute(panels, both, [(i, i ^ 1) for i in range(count) if not waits(i)])
    inside = lax.ppermute(panels, both, swaps(lambda i: not crosses(i)))
    across = lax.ppermute(panels, both, swaps(lambda i: crosses(i) and not wraps(i)))
    blocks = level(2, blocks, partner)
    gathered = exchange_pairs(blocks, "row", 1 << (row_bits - 2))
    return last_and_near(
        3,
        own_bit + row_bits - 2,
        (pattern, octree_order, neighbors),
        blocks,
        gathered,
        matrices,
        (early, paired, panels, inside, wrapped, across),
        near_blocks,
    )


def solution(mesh):
    in_specs = (
        P(None, ("row", "col")),
        P(None, ("row", "col"), None, None),
        P(None, ("row", "col")),
        P(("row", "col")),
        P(None, ("row", "col")),
        P(("row", "col"), None, None, None),
        P(("row", "col"), None),
    )
    out_specs = (P(None, ("row", "col")), P(None, ("row", "col")))
    return jax.shard_map(
        per_device, mesh=mesh, in_specs=in_specs, out_specs=out_specs, check_vma=False
    )
```
